256 devices in a mesh: lat: 32 (over y_lo, z, core), lon: 8 (over x, y_hi).
Axes of the slice: x: 4, y: 4 (y_hi: 2, y_lo: 2; y = y_hi * 2 + y_lo), z: 8, core: 2. Of those that a mesh axis runs over, the one named last changes fastest.
Arguments:
- signal: bfloat16 [768, 64, 1024], P(None, 'lat', 'lon'), may hold values from -6 to 6
- gate_input: bfloat16 [768, 64, 1024], P(None, 'lat', 'lon'), may hold values from -6 to 6
- cotangent: bfloat16 [768, 64, 1024], P(None, 'lat', 'lon'), may hold values from -6 to 6
- zonal_taps: bfloat16 [768, 256], P('lat'), may hold values from -0.375 to 0.375
- meridional_taps: float32 [768, 128], P('lat'), may hold values from -0.75 to 0.75
Outputs:
- mixed: bfloat16 [768, 64, 1024], P(None, 'lat', 'lon')
- gate_grad: bfloat16 [768, 64, 1024], P(None, 'lat', 'lon')
- signal_grad: bfloat16 [768, 64, 1024], P(None, 'lat', 'lon')
- zonal_grad: float32 [768, 256], P('lat')
- meridional_grad: float32 [768, 128], P('lat')
The draws below stay inside these ranges and needn't reach their ends.
All inputs are finite; a program needn't handle non-finite values.
Results may differ from the reference program's by a relative error of at most 0.015.
Values may be sent and summed in bfloat16 or wider, within the bound.
A program may use at most 64 MiB of HBM per device.

```python
import jax
import jax.numpy as jnp
from jax import lax

CHANNELS = 768
REACH = 128
NLAT = 64
NLON = 1024
PADDED = 128
TAPS = 256


def levels(own_key, dims, cuts, least, high):
    def one(position, parts):
        heights = jax.random.uniform(jax.random.fold_in(jax.random.fold_in(own_key, 6), position), (parts,), jnp.float32, least / len(cuts), high / len(cuts))
        return jnp.repeat(jnp.exp(heights), dims[position] // parts).reshape((-1,) + (1,) * (len(dims) - position - 1))

    loudness = one(*cuts[0])
    for cut in cuts[1:]:
        loudness = loudness * one(*cut)
    return loudness


def bell_draw(own_key, shape, spread, limit, cuts=(), dtype=jnp.bfloat16):
    loudness = levels(own_key, shape, cuts, -0.22, 0.18) if cuts else 1.0
    drawn = jax.random.normal(own_key, shape, jnp.float32) * spread * loudness
    return jnp.minimum(jnp.maximum(drawn, -limit), limit).astype(dtype)


def setup_inputs(seed: int = 0) -> dict:
    key_list = jax.random.split(jax.random.key(seed), 6)
    signal = bell_draw(key_list[0], (CHANNELS, NLAT, NLON), 1.0, 6.0, ((1, 32), (2, 8)))
    gate_input = bell_draw(key_list[1], (CHANNELS, NLAT, NLON), 1.0, 6.0, ((1, 32), (2, 8)))
    cotangent = bell_draw(key_list[2], (CHANNELS, NLAT, NLON), 1.0, 6.0, ((1, 32), (2, 8)))
    zonal_taps = bell_draw(key_list[3], (CHANNELS, TAPS), TAPS ** -0.5, 0.375, ((0, 32),))
    meridional_taps = bell_draw(key_list[4], (CHANNELS, PADDED), NLAT ** -0.5, 0.75, ((0, 32),), jnp.float32)
    return dict(signal=signal, gate_input=gate_input, cotangent=cotangent, zonal_taps=zonal_taps, meridional_taps=meridional_taps)


def one_channel(fields):
    signal, gate_input, cotangent, zonal, meridional = fields
    signal_float = signal.astype(jnp.float32)
    gate_float = gate_input.astype(jnp.float32)
    grad_float = cotangent.astype(jnp.float32)
    circle = jnp.roll(jnp.pad(zonal.astype(jnp.float32), (0, NLON - TAPS)), -REACH)
    circle_spec = jnp.fft.rfft(circle)
    signal_spec = jnp.fft.rfft(signal_float, axis=1)
    filtered = jnp.fft.irfft(signal_spec * circle_spec[None, :], n=NLON, axis=1)
    taps_spec = jnp.fft.rfft(meridional)
    filtered_spec = jnp.fft.rfft(filtered, n=PADDED, axis=0)
    convolved = jnp.fft.irfft(filtered_spec * taps_spec[:, None], n=PADDED, axis=0)[:NLAT]
    convolved_round = lax.optimization_barrier(convolved.astype(jnp.bfloat16)).astype(jnp.float32)
    mixed = (gate_float * convolved_round).astype(jnp.bfloat16)
    gate_grad = (grad_float * convolved_round).astype(jnp.bfloat16)
    conv_grad = lax.optimization_barrier((grad_float * gate_float).astype(jnp.bfloat16)).astype(jnp.float32)
    conv_spec = jnp.fft.rfft(conv_grad, n=PADDED, axis=0)
    filtered_grad = jnp.fft.irfft(jnp.conj(taps_spec)[:, None] * conv_spec, n=PADDED, axis=0)[:NLAT]
    rounded_grad = filtered_grad.astype(jnp.bfloat16)
    grad_back = lax.optimization_barrier(rounded_grad).astype(jnp.float32)
    grad_spec = jnp.fft.rfft(grad_back, axis=1)
    signal_grad = jnp.fft.irfft(grad_spec * jnp.conj(circle_spec)[None, :], n=NLON, axis=1).astype(jnp.bfloat16)
    scale = 1.0 / jnp.sqrt(jnp.float32(NLAT * NLON))
    cross_lon = lax.optimization_barrier(jnp.sum(grad_spec * jnp.conj(signal_spec), axis=0))
    corr_lon = jnp.fft.irfft(cross_lon, n=NLON)
    zonal_grad = jnp.roll(corr_lon, REACH)[:TAPS] * scale
    cross_lat = lax.optimization_barrier(jnp.sum(conv_spec * jnp.conj(filtered_spec), axis=1))
    meridional_grad = jnp.fft.irfft(cross_lat, n=PADDED) * scale
    return (mixed, gate_grad, signal_grad, zonal_grad.astype(jnp.float32), meridional_grad.astype(jnp.float32))

def reference(signal, gate_input, cotangent, zonal_taps, meridional_taps):
    results = lax.map(one_channel, (signal, gate_input, cotangent, zonal_taps, meridional_taps))
    return (results[0], results[1], results[2], results[3], results[4])
```

```python
import jax
import jax.numpy as jnp
from jax import lax
from jax.experimental import pallas as pl
from jax.experimental.pallas import tpu as pltpu
from jax.sharding import PartitionSpec as P

MESH = pl.DeviceIdType.MESH
BF16 = jnp.bfloat16
F32 = jnp.float32
LATS, LONS = 32, 8
CHANNELS = 768
GROUP = 24
OWN = 3
ROWS = 64
COLS = 128
Z_STEPS = (1, 7, 2, 6, 3, 5, 4, 0)


def dot(a, b, a_dim=1, b_dim=0):
    return lax.dot_general(
        a, b, (((a_dim,), (b_dim,)), ((), ())), preferred_element_type=F32
    )


def place():
    lat, lon = lax.axis_index("lat"), lax.axis_index("lon")
    return lat, lon


def each_peer(lat, lon, visit):
    y_lo, z, core = lat // 16, (lat // 2) % 8, lat % 2
    x, y = lon // 2, (lon % 2) * 2 + y_lo

    def around(i, carry):
        x_peer, y_peer = (x + i % 4) % 4, (y + (i // 4) % 4) % 4
        lat_base = (y_peer % 2) * 16 + (core + i // 16) % 2
        lon_peer = x_peer * 2 + y_peer // 2
        for step in Z_STEPS:
            lat_peer = lat_base + ((z + step) % 8) * 2
            if step:
                visit(lat_peer, lon_peer)
            else:

                @pl.when(i != 0)
                def _():
                    visit(lat_peer, lon_peer)

        return carry

    lax.fori_loop(0, 32, around, 0)


def reversal(size):
    rows = lax.broadcasted_iota(jnp.int32, (size, size), 0)
    cols = lax.broadcasted_iota(jnp.int32, (size, size), 1)
    return jnp.where(rows + cols == size - 1, 1.0, 0.0).astype(BF16)


def around_circle(blocks):
    return jnp.concatenate(
        [
            jnp.concatenate([blocks[(b + d - 1) % LONS] for d in range(3)], axis=1)
            for b in range(LONS)
        ],
        axis=0,
    )


def mixer(
    signal,
    gate,
    cotangent,
    zonal,
    meridional,
    conv_out,
    grad_out,
    zonal_out,
    meridional_out,
    zonal_rows,
    grad_src,
    signal_in,
    grad_in,
    conv_src,
    result_src,
    ahead,
    back,
    lat_weights,
    taps_src,
    taps_in,
    send,
    recv,
):
    lat, lon = place()
    mine = lat * GROUP + lon * OWN
    barrier = pltpu.get_barrier_semaphore()

    def greet(lat_peer, lon_peer):
        pl.semaphore_signal(
            barrier, inc=1, device_id=(lat_peer, lon_peer), device_id_type=MESH
        )

    each_peer(lat, lon, greet)

    flat = (CHANNELS * 2, COLS)
    product = gate.reshape(*flat)[...].astype(F32) * cotangent.reshape(*flat)[...].astype(F32)
    grad_src.reshape(*flat)[...] = product.astype(BF16)

    pl.semaphore_wait(barrier, LATS * LONS - 1)

    def spread(source, landing, k):
        def to(lat_peer, lon_peer):
            pltpu.make_async_remote_copy(
                source.at[pl.ds(lat_peer * GROUP + lon_peer * OWN, OWN)],
                landing.at[lon, :, lat],
                send.at[k],
                recv.at[k],
                device_id=(lat_peer, lon_peer),
                device_id_type=MESH,
            ).start()

        each_peer(lat, lon, to)
        landing[lon, :, lat] = source[pl.ds(mine, OWN)]

    def give_back(source, landing, k):
        def to(lat_peer, lon_peer):
            pltpu.make_async_remote_copy(
                source.at[lon_peer, :, lat_peer],
                landing.at[pl.ds(mine, OWN)],
                send.at[k],
                recv.at[k],
                device_id=(lat_peer, lon_peer),
                device_id_type=MESH,
            ).start()

        each_peer(lat, lon, to)
        landing[pl.ds(mine, OWN)] = source[lon, :, lat]

    others = signal.at[pl.ds(0, CHANNELS - OWN)]

    def wait_for(semaphore):
        pltpu.make_async_copy(others, others, semaphore).wait()

    spread(signal, signal_in, 0)
    spread(grad_src, grad_in, 1)

    zonal_rows[...] = zonal[...].astype(F32)
    for j in range(OWN):
        row = jnp.concatenate(
            [zonal_rows[pl.ds(lon * OWN + j, 1), :], jnp.zeros((1, 256), F32)], axis=1
        )
        skew = pltpu.roll(
            jnp.broadcast_to(row, (COLS, 512)), 0, 1, stride=1, stride_axis=0
        )
        for d in range(3):
            block = skew[:, 256 - 128 * d : 384 - 128 * d]
            ahead[j, d * COLS : (d + 1) * COLS, :] = block.astype(BF16)
            back[j, (2 - d) * COLS : (3 - d) * COLS, :] = block.T.astype(BF16)
        line = meridional[pl.ds(lon * OWN + j, 1), :]
        turned = pltpu.roll(
            jnp.broadcast_to(line, (ROWS, COLS)), 0, 1, stride=1, stride_axis=0
        )
        lat_weights[j] = turned.astype(BF16)
    flip_cols, flip_rows = reversal(COLS), reversal(ROWS)

    signal_view = signal_in.reshape(LONS, OWN, ROWS, COLS)
    grad_view = grad_in.reshape(LONS, OWN, ROWS, COLS)
    conv_view = conv_src.reshape(LONS, OWN, ROWS, COLS)
    result_view = result_src.reshape(LONS, OWN, ROWS, COLS)

    wait_for(recv.at[0])
    backwards, flipped = [], []
    for j in range(OWN):
        blocks = [signal_view[b, j] for b in range(LONS)]
        filtered = dot(around_circle(blocks), ahead[j]).astype(BF16)
        wide = jnp.concatenate(
            [filtered[b * ROWS : (b + 1) * ROWS] for b in range(LONS)], axis=1
        )
        convolved = dot(lat_weights[j][:, :ROWS], wide, 0, 0).astype(BF16)
        for b in range(LONS):
            conv_view[b, j] = convolved[:, b * COLS : (b + 1) * COLS]
        flipped.append(dot(flip_rows, wide).astype(BF16))
    give_back(conv_src, conv_out, 2)
    for j in range(OWN):
        stack = jnp.concatenate([signal_view[b, j] for b in range(LONS)], axis=0)
        turned = dot(stack, flip_cols).astype(BF16)
        backwards.append([turned[b * ROWS : (b + 1) * ROWS] for b in range(LONS)])

    wait_for(recv.at[1])
    rounded = []
    for j in range(OWN):
        wide = jnp.concatenate([grad_view[b, j] for b in range(LONS)], axis=1)
        gradient = dot(lat_weights[j][:, :ROWS], wide).astype(BF16)
        blocks = [gradient[:, b * COLS : (b + 1) * COLS] for b in range(LONS)]
        rounded.append(jnp.concatenate(blocks, axis=0))
        result = dot(around_circle(blocks), back[j]).astype(BF16)
        for b in range(LONS):
            result_view[b, j] = result[b * ROWS : (b + 1) * ROWS]
    give_back(result_src, grad_out, 3)

    scale = 1.0 / 256.0
    for j in range(OWN):
        products = dot(around_circle(backwards[j]), rounded[j], 0, 0)
        side = jnp.concatenate(
            [products[2 * COLS :], products[COLS : 2 * COLS], products[:COLS], jnp.zeros((COLS, COLS), F32)],
            axis=1,
        )
        diagonals = pltpu.roll(side, 385, 1, stride=1, stride_axis=0)
        taps_src[pl.ds(j, 1), :256] = (
            jnp.sum(diagonals[:, :256], axis=0, keepdims=True) * scale
        )
        wide = jnp.concatenate([grad_view[b, j] for b in range(LONS)], axis=1)
        crossed = dot(flipped[j], wide, 1, 1)
        crossed = jnp.concatenate([crossed, jnp.zeros((ROWS, ROWS), F32)], axis=1)
        diagonals = pltpu.roll(crossed, 65, 1, stride=1, stride_axis=0)
        taps_src[pl.ds(j, 1), 256:] = jnp.sum(diagonals, axis=0, keepdims=True) * scale
    for step in range(1, LONS):
        pltpu.make_async_remote_copy(
            taps_src,
            taps_in.at[lon],
            send.at[4],
            recv.at[4],
            device_id=(lat, (lon + step) % LONS),
            device_id_type=MESH,
        ).start()
    taps_in[lon] = taps_src[...]

    seven = taps_in.at[pl.ds(0, LONS - 1)]
    pltpu.make_async_copy(seven, seven, recv.at[4]).wait()
    for b in range(LONS):
        for j in range(OWN):
            zonal_out[b * OWN + j : b * OWN + j + 1, :] = taps_in[b, j : j + 1, :256]
            meridional_out[b * OWN + j : b * OWN + j + 1, :] = taps_in[b, j : j + 1, 256:]

    wait_for(recv.at[2])
    wait_for(recv.at[3])
    for k in range(4):
        wait_for(send.at[k])
    pltpu.make_async_copy(seven, seven, send.at[4]).wait()


def on_device(signal, gate, cotangent, zonal, meridional):
    field = (CHANNELS, 2, COLS)
    pencil = (LONS, OWN, LATS, 2, COLS)
    in_vmem = pl.BlockSpec(memory_space=pltpu.VMEM)
    convolved, signal_grad, zonal_grad, meridional_grad = pl.pallas_call(
        mixer,
        out_shape=[
            jax.ShapeDtypeStruct(field, BF16),
            jax.ShapeDtypeStruct(field, BF16),
            jax.ShapeDtypeStruct((GROUP, 256), F32),
            jax.ShapeDtypeStruct((GROUP, 128), F32),
        ],
        in_specs=[in_vmem] * 5,
        out_specs=[in_vmem] * 4,
        scratch_shapes=[
            pltpu.VMEM((GROUP, 256), F32),
            pltpu.VMEM(field, BF16),
            pltpu.VMEM(pencil, BF16),
            pltpu.VMEM(pencil, BF16),
            pltpu.VMEM(pencil, BF16),
            pltpu.VMEM(pencil, BF16),
            pltpu.VMEM((OWN, 3 * COLS, COLS), BF16),
            pltpu.VMEM((OWN, 3 * COLS, COLS), BF16),
            pltpu.VMEM((OWN, ROWS, COLS), BF16),
            pltpu.VMEM((8, 384), F32),
            pltpu.VMEM((LONS, 8, 384), F32),
            pltpu.SemaphoreType.DMA((5,)),
            pltpu.SemaphoreType.DMA((5,)),
        ],
        compiler_params=pltpu.CompilerParams(
            collective_id=0, has_side_effects=True, vmem_limit_bytes=32 * 1024 * 1024
        ),
        name="mixer",
    )(signal, gate, cotangent, zonal, meridional)
    wide = convolved.astype(F32)
    mixed = (gate.astype(F32) * wide).astype(BF16)
    gate_grad = (cotangent.astype(F32) * wide).astype(BF16)
    return mixed, gate_grad, signal_grad, zonal_grad, meridional_grad


def solution(mesh):
    fields = P(None, "lat", "lon")
    filters = P("lat", None)
    return jax.shard_map(
        on_device,
        mesh=mesh,
        in_specs=(fields, fields, fields, filters, filters),
        out_specs=(fields, fields, fields, filters, filters),
        check_vma=False,
    )
```

```python
import jax
import jax.numpy as jnp
from jax import lax
from jax.experimental import pallas as pl
from jax.experimental.pallas import tpu as pltpu
from jax.sharding import PartitionSpec as P

MESH = pl.DeviceIdType.MESH
BF16 = jnp.bfloat16
F32 = jnp.float32
LATS, LONS = 32, 8
CHANNELS = 768
GROUP = 24
VMEM_BYTES = 60 * 1024 * 1024
OWN = 3
ROWS = 64
COLS = 128
Z_STEPS = (4, 3, 5, 2, 6, 1, 7)


def dot(a, b, a_dim=1, b_dim=0):
    return lax.dot_general(
        a, b, (((a_dim,), (b_dim,)), ((), ())), preferred_element_type=F32
    )


def place():
    lat, lon = lax.axis_index("lat"), lax.axis_index("lon")
    return lat, lon


def each_peer(lat, lon, visit):
    y_lo, z, core = lat // 16, (lat // 2) % 8, lat % 2
    x, y = lon // 2, (lon % 2) * 2 + y_lo

    def towards(i):
        x_peer, y_peer = (x + i % 4) % 4, (y + (i // 4) % 4) % 4
        return (y_peer % 2) * 16 + (core + i // 16) % 2, x_peer * 2 + y_peer // 2

    def other_planes(i, carry):
        lat_base, lon_peer = towards(i)
        for step in Z_STEPS:
            visit(lat_base + ((z + step) % 8) * 2, lon_peer)
        return carry

    def own_plane(i, carry):
        lat_base, lon_peer = towards(i)
        visit(lat_base + z * 2, lon_peer)
        return carry

    lax.fori_loop(0, 32, other_planes, 0)
    lax.fori_loop(1, 32, own_plane, 0)


def neighbours(lat, lon):
    y_lo, z, core = lat // 16, (lat // 2) % 8, lat % 2
    x, y = lon // 2, (lon % 2) * 2 + y_lo
    column = [
        (y_lo * 16 + ((z + step) % 8) * 2 + (core + other) % 2, lon)
        for other in (1, 0)
        for step in Z_STEPS + (0,)
        if step or other
    ]
    plane = []
    for y_step in (1, 3, 2, 0):
        for x_step in (1, 3, 2, 0):
            if x_step or y_step:
                x_peer, y_peer = (x + x_step) % 4, (y + y_step) % 4
                plane.append(
                    ((y_peer % 2) * 16 + z * 2 + core, x_peer * 2 + y_peer // 2)
                )
    return column, plane


def reversal(size):
    rows = lax.broadcasted_iota(jnp.int32, (size, size), 0)
    cols = lax.broadcasted_iota(jnp.int32, (size, size), 1)
    return jnp.where(rows + cols == size - 1, 1.0, 0.0).astype(BF16)


def around_circle(blocks):
    return jnp.concatenate(
        [
            jnp.concatenate([blocks[(b + d - 1) % LONS] for d in range(3)], axis=1)
            for b in range(LONS)
        ],
        axis=0,
    )


def mixer(
    signal_hbm,
    gate_hbm,
    cotangent_hbm,
    zonal_hbm,
    meridional_hbm,
    mixed_out,
    gate_out,
    grad_out,
    zonal_out,
    meridional_out,
    signal,
    gate,
    cotangent,
    zonal,
    meridional,
    conv_in,
    mixed,
    gate_grad,
    zonal_rows,
    grad_src,
    signal_in,
    grad_in,
    conv_src,
    result_src,
    ahead,
    back,
    lat_weights,
    taps_src,
    taps_in,
    send,
    recv,
    load,
    ready,
):
    lat, lon = place()
    mine = lat * GROUP + lon * OWN
    column, plane = neighbours(lat, lon)
    barrier = pltpu.get_barrier_semaphore()
    for peer in column + plane:
        pl.semaphore_signal(barrier, inc=1, device_id=peer, device_id_type=MESH)

    loads = [
        pltpu.make_async_copy(source, target, load.at[k])
        for k, (source, target) in enumerate(
            (
                (gate_hbm, gate),
                (cotangent_hbm, cotangent),
                (signal_hbm, signal),
                (zonal_hbm, zonal),
                (meridional_hbm, meridional),
            )
        )
    ]
    for copy in loads:
        copy.start()
    loads[0].wait()
    loads[1].wait()
    flat = (CHANNELS * 2, COLS)
    gate_flat, cotangent_flat = gate.reshape(*flat), cotangent.reshape(*flat)
    product = gate_flat[...].astype(F32) * cotangent_flat[...].astype(F32)
    grad_src.reshape(*flat)[...] = product.astype(BF16)
    for copy in loads[2:]:
        copy.wait()

    pl.semaphore_wait(barrier, len(column) + len(plane))
    for peer in plane:
        pl.semaphore_signal(ready, inc=1, device_id=peer, device_id_type=MESH)
    pl.semaphore_wait(ready, len(plane))

    def spread(source, landing, k):
        def to(lat_peer, lon_peer):
            pltpu.make_async_remote_copy(
                source.at[pl.ds(lat_peer * GROUP + lon_peer * OWN, OWN)],
                landing.at[lon, :, lat],
                send.at[k],
                recv.at[k],
                device_id=(lat_peer, lon_peer),
                device_id_type=MESH,
            ).start()

        each_peer(lat, lon, to)
        landing[lon, :, lat] = source[pl.ds(mine, OWN)]

    def give_back(source, landing, k):
        def to(lat_peer, lon_peer):
            pltpu.make_async_remote_copy(
                source.at[lon_peer, :, lat_peer],
                landing.at[pl.ds(mine, OWN)],
                send.at[k],
                recv.at[k],
                device_id=(lat_peer, lon_peer),
                device_id_type=MESH,
            ).start()

        each_peer(lat, lon, to)
        return pltpu.make_async_copy(
            source.at[lon, :, lat], landing.at[pl.ds(mine, OWN)], load.at[k]
        )

    others = signal.at[pl.ds(0, CHANNELS - OWN)]

    def wait_for(semaphore):
        pltpu.make_async_copy(others, others, semaphore).wait()

    spread(signal, signal_in, 0)
    spread(grad_src, grad_in, 1)

    zonal_rows[...] = zonal[...].astype(F32)
    for j in range(OWN):
        row = jnp.concatenate(
            [zonal_rows[pl.ds(lon * OWN + j, 1), :], jnp.zeros((1, 256), F32)], axis=1
        )
        skew = pltpu.roll(
            jnp.broadcast_to(row, (COLS, 512)), 0, 1, stride=1, stride_axis=0
        )
        for d in range(3):
            block = skew[:, 256 - 128 * d : 384 - 128 * d]
            ahead[j, d * COLS : (d + 1) * COLS, :] = block.astype(BF16)
            back[j, (2 - d) * COLS : (3 - d) * COLS, :] = block.T.astype(BF16)
        line = meridional[pl.ds(lon * OWN + j, 1), :]
        turned = pltpu.roll(
            jnp.broadcast_to(line, (ROWS, COLS)), 0, 1, stride=1, stride_axis=0
        )
        lat_weights[j] = turned.astype(BF16)
    flip_cols, flip_rows = reversal(COLS), reversal(ROWS)

    signal_view = signal_in.reshape(LONS, OWN, ROWS, COLS)
    grad_view = grad_in.reshape(LONS, OWN, ROWS, COLS)
    conv_view = conv_src.reshape(LONS, OWN, ROWS, COLS)
    result_view = result_src.reshape(LONS, OWN, ROWS, COLS)

    wait_for(recv.at[0])
    backwards, flipped = [], []
    for j in range(OWN):
        blocks = [signal_view[b, j] for b in range(LONS)]
        filtered = dot(around_circle(blocks), ahead[j]).astype(BF16)
        wide = jnp.concatenate(
            [filtered[b * ROWS : (b + 1) * ROWS] for b in range(LONS)], axis=1
        )
        convolved = dot(lat_weights[j][:, :ROWS], wide, 0, 0).astype(BF16)
        for b in range(LONS):
            conv_view[b, j] = convolved[:, b * COLS : (b + 1) * COLS]
        flipped.append(dot(flip_rows, wide).astype(BF16))
    own_conv = give_back(conv_src, conv_in, 2)
    own_conv.start()
    for j in range(OWN):
        stack = jnp.concatenate([signal_view[b, j] for b in range(LONS)], axis=0)
        turned = dot(stack, flip_cols).astype(BF16)
        backwards.append([turned[b * ROWS : (b + 1) * ROWS] for b in range(LONS)])

    wait_for(recv.at[1])
    rounded = []
    for j in range(OWN):
        wide = jnp.concatenate([grad_view[b, j] for b in range(LONS)], axis=1)
        gradient = dot(lat_weights[j][:, :ROWS], wide).astype(BF16)
        blocks = [gradient[:, b * COLS : (b + 1) * COLS] for b in range(LONS)]
        rounded.append(jnp.concatenate(blocks, axis=0))
        result = dot(around_circle(blocks), back[j]).astype(BF16)
        for b in range(LONS):
            result_view[b, j] = result[b * ROWS : (b + 1) * ROWS]
    own_grad = give_back(result_src, grad_out, 3)
    own_grad.start()

    scale = 1.0 / 256.0
    for j in range(OWN):
        products = dot(around_circle(backwards[j]), rounded[j], 0, 0)
        side = jnp.concatenate(
            [products[2 * COLS :], products[COLS : 2 * COLS], products[:COLS], jnp.zeros((COLS, COLS), F32)],
            axis=1,
        )
        diagonals = pltpu.roll(side, 385, 1, stride=1, stride_axis=0)
        taps_src[pl.ds(j, 1), :256] = (
            jnp.sum(diagonals[:, :256], axis=0, keepdims=True) * scale
        )
        wide = jnp.concatenate([grad_view[b, j] for b in range(LONS)], axis=1)
        crossed = dot(flipped[j], wide, 1, 1)
        crossed = jnp.concatenate([crossed, jnp.zeros((ROWS, ROWS), F32)], axis=1)
        diagonals = pltpu.roll(crossed, 65, 1, stride=1, stride_axis=0)
        taps_src[pl.ds(j, 1), 256:] = jnp.sum(diagonals, axis=0, keepdims=True) * scale
    for step in range(1, LONS):
        pltpu.make_async_remote_copy(
            taps_src,
            taps_in.at[lon],
            send.at[4],
            recv.at[4],
            device_id=(lat, (lon + step) % LONS),
            device_id_type=MESH,
        ).start()
    taps_in[lon] = taps_src[...]

    seven = taps_in.at[pl.ds(0, LONS - 1)]
    pltpu.make_async_copy(seven, seven, recv.at[4]).wait()
    for b in range(LONS):
        for j in range(OWN):
            zonal_out[b * OWN + j : b * OWN + j + 1, :] = taps_in[b, j : j + 1, :256]
            meridional_out[b * OWN + j : b * OWN + j + 1, :] = taps_in[b, j : j + 1, 256:]

    own_conv.wait()
    wait_for(recv.at[2])
    convolved = conv_in.reshape(*flat)[...].astype(F32)
    mixed.reshape(*flat)[...] = (gate_flat[...].astype(F32) * convolved).astype(BF16)
    gate_grad.reshape(*flat)[...] = (cotangent_flat[...].astype(F32) * convolved).astype(BF16)
    stores = [
        pltpu.make_async_copy(mixed, mixed_out, load.at[0]),
        pltpu.make_async_copy(gate_grad, gate_out, load.at[1]),
    ]
    for copy in stores:
        copy.start()
    for copy in stores + [own_grad]:
        copy.wait()
    wait_for(recv.at[3])
    for k in range(4):
        wait_for(send.at[k])
    pltpu.make_async_copy(seven, seven, send.at[4]).wait()


def place_results(*refs):
    made, placed, held, (arrived, left) = refs[:5], refs[5:10], refs[10:15], refs[15:]
    loads = [
        pltpu.make_async_copy(made[k], held[k], arrived.at[k]) for k in range(len(made))
    ]
    stores = [
        pltpu.make_async_copy(held[k], placed[k], left.at[k]) for k in range(len(made))
    ]
    for copy in loads:
        copy.start()
    for load, store in zip(loads, stores):
        load.wait()
        store.start()
    for copy in stores:
        copy.wait()


def on_device(signal, gate, cotangent, zonal, meridional):
    field = (CHANNELS, 2, COLS)
    pencil = (LONS, OWN, LATS, 2, COLS)
    in_vmem = pl.BlockSpec(memory_space=pltpu.VMEM)
    in_hbm = pl.BlockSpec(memory_space=pltpu.HBM)
    results = [
        jax.ShapeDtypeStruct(field, BF16),
        jax.ShapeDtypeStruct(field, BF16),
        jax.ShapeDtypeStruct(field, BF16),
        jax.ShapeDtypeStruct((GROUP, 256), F32),
        jax.ShapeDtypeStruct((GROUP, 128), F32),
    ]
    made = pl.pallas_call(
        mixer,
        out_shape=results,
        in_specs=[in_hbm] * 5,
        out_specs=[in_hbm] * 3 + [in_vmem] * 2,
        scratch_shapes=[
            pltpu.VMEM(field, BF16),
            pltpu.VMEM(field, BF16),
            pltpu.VMEM(field, BF16),
            pltpu.VMEM((GROUP, 256), BF16),
            pltpu.VMEM((GROUP, 128), F32),
            pltpu.VMEM(field, BF16),
            pltpu.VMEM(field, BF16),
            pltpu.VMEM(field, BF16),
            pltpu.VMEM((GROUP, 256), F32),
            pltpu.VMEM(field, BF16),
            pltpu.VMEM(pencil, BF16),
            pltpu.VMEM(pencil, BF16),
            pltpu.VMEM(pencil, BF16),
            pltpu.VMEM(pencil, BF16),
            pltpu.VMEM((OWN, 3 * COLS, COLS), BF16),
            pltpu.VMEM((OWN, 3 * COLS, COLS), BF16),
            pltpu.VMEM((OWN, ROWS, COLS), BF16),
            pltpu.VMEM((8, 384), F32),
            pltpu.VMEM((LONS, 8, 384), F32),
            pltpu.SemaphoreType.DMA((5,)),
            pltpu.SemaphoreType.DMA((5,)),
            pltpu.SemaphoreType.DMA((5,)),
            pltpu.SemaphoreType.REGULAR,
        ],
        compiler_params=pltpu.CompilerParams(
            collective_id=0, has_side_effects=True, vmem_limit_bytes=VMEM_BYTES
        ),
        name="mixer",
    )(signal, gate, cotangent, zonal, meridional)
    return pl.pallas_call(
        place_results,
        out_shape=results,
        in_specs=[in_hbm] * 5,
        out_specs=[in_hbm] * 5,
        scratch_shapes=[pltpu.VMEM(shape.shape, shape.dtype) for shape in results]
        + [pltpu.SemaphoreType.DMA((5,)), pltpu.SemaphoreType.DMA((5,))],
        compiler_params=pltpu.CompilerParams(vmem_limit_bytes=VMEM_BYTES),
        name="place_results",
    )(*made)


def solution(mesh):
    fields = P(None, "lat", "lon")
    filters = P("lat", None)
    return jax.shard_map(
        on_device,
        mesh=mesh,
        in_specs=(fields, fields, fields, filters, filters),
        out_specs=(fields, fields, fields, filters, filters),
        check_vma=False,
    )
```

```python
import jax
import jax.numpy as jnp
from jax import lax
from jax.experimental import pallas as pl
from jax.experimental.pallas import tpu as pltpu
from jax.sharding import PartitionSpec as P

MESH = pl.DeviceIdType.MESH
BF16 = jnp.bfloat16
F32 = jnp.float32
LATS, LONS = 32, 8
CHANNELS = 768
GROUP = 24
VMEM_BYTES = 32 * 1024 * 1024
OWN = 3
ROWS = 64
COLS = 128
Z_STEPS = (4, 3, 5, 2, 6, 1, 7)


def dot(a, b, a_dim=1, b_dim=0):
    return lax.dot_general(
        a, b, (((a_dim,), (b_dim,)), ((), ())), preferred_element_type=F32
    )


def place():
    lat, lon = lax.axis_index("lat"), lax.axis_index("lon")
    return lat, lon


def each_peer(lat, lon, visit, first=True, rest=True):
    if first:
        column, plane = neighbours(lat, lon)
        for peer in column + plane:
            visit(*peer)
    if not rest:
        return
    y_lo, z, core = lat // 16, (lat // 2) % 8, lat % 2
    x, y = lon // 2, (lon % 2) * 2 + y_lo

    def toward(i, steps, same_core):
        x_peer, y_peer = (x + i % 4) % 4, (y + i // 4) % 4
        core_peer = core if same_core else 1 - core
        lat_base = (y_peer % 2) * 16 + core_peer
        for step in steps:
            visit(lat_base + ((z + step) % 8) * 2, x_peer * 2 + y_peer // 2)

    for steps in ((4,), (3, 5), (2, 6), (1, 7), (0,)):

        def around(i, carry):
            if steps != (0,):
                toward(i, steps, True)
            toward(i, steps, False)
            return carry

        lax.fori_loop(1, 16, around, 0)


def neighbours(lat, lon):
    y_lo, z, core = lat // 16, (lat // 2) % 8, lat % 2
    x, y = lon // 2, (lon % 2) * 2 + y_lo
    column = [
        (y_lo * 16 + ((z + step) % 8) * 2 + (core + other) % 2, lon)
        for other in (1, 0)
        for step in Z_STEPS + (0,)
        if step or other
    ]
    plane = []
    for y_step in (1, 3, 2, 0):
        for x_step in (1, 3, 2, 0):
            if x_step or y_step:
                x_peer, y_peer = (x + x_step) % 4, (y + y_step) % 4
                plane.append(
                    ((y_peer % 2) * 16 + z * 2 + core, x_peer * 2 + y_peer // 2)
                )
    return column, plane


def reversal(size):
    rows = lax.broadcasted_iota(jnp.int32, (size, size), 0)
    cols = lax.broadcasted_iota(jnp.int32, (size, size), 1)
    return jnp.where(rows + cols == size - 1, 1.0, 0.0).astype(BF16)


def around_circle(blocks):
    return jnp.concatenate(
        [
            jnp.concatenate([blocks[(b + d - 1) % LONS] for d in range(3)], axis=1)
            for b in range(LONS)
        ],
        axis=0,
    )


def mixer(
    signal,
    gate_hbm,
    cotangent_hbm,
    zonal_hbm,
    meridional_hbm,
    mixed_out,
    gate_out,
    grad_out,
    zonal_out,
    meridional_out,
    gate,
    cotangent,
    zonal,
    meridional,
    conv_in,
    zonal_rows,
    grad_src,
    signal_in,
    grad_in,
    conv_src,
    result_src,
    ahead,
    back,
    lat_weights,
    taps_src,
    taps_in,
    send,
    recv,
    load,
    ready,
):
    lat, lon = place()
    mine = lat * GROUP + lon * OWN
    column, plane = neighbours(lat, lon)
    barrier = pltpu.get_barrier_semaphore()
    for peer in column + plane:
        pl.semaphore_signal(barrier, inc=1, device_id=peer, device_id_type=MESH)

    loads = [
        pltpu.make_async_copy(source, target, load.at[k])
        for k, (source, target) in enumerate(
            (
                (gate_hbm, gate),
                (cotangent_hbm, cotangent),
                (signal.at[pl.ds(mine, OWN)], signal_in.at[lon, :, lat]),
                (zonal_hbm, zonal),
                (meridional_hbm, meridional),
            )
        )
    ]
    for copy in loads:
        copy.start()

    pl.semaphore_wait(barrier, len(column) + len(plane))
    for peer in plane:
        pl.semaphore_signal(ready, inc=1, device_id=peer, device_id_type=MESH)

    def spread(source, landing, k, **which):
        def to(lat_peer, lon_peer):
            pltpu.make_async_remote_copy(
                source.at[pl.ds(lat_peer * GROUP + lon_peer * OWN, OWN)],
                landing.at[lon, :, lat],
                send.at[k],
                recv.at[k],
                device_id=(lat_peer, lon_peer),
                device_id_type=MESH,
            ).start()

        each_peer(lat, lon, to, **which)

    spread(signal, signal_in, 0, rest=False)
    for copy in loads:
        copy.wait()
    flat = (CHANNELS * 2, COLS)
    gate_flat, cotangent_flat = gate.reshape(*flat), cotangent.reshape(*flat)
    product = gate_flat[...].astype(F32) * cotangent_flat[...].astype(F32)
    grad_src.reshape(*flat)[...] = product.astype(BF16)
    spread(grad_src, grad_in, 1, rest=False)
    grad_in[lon, :, lat] = grad_src[pl.ds(mine, OWN)]

    pl.semaphore_wait(ready, len(plane))
    spread(signal, signal_in, 0, first=False)
    spread(grad_src, grad_in, 1, first=False)

    def give_back(source, landing, k):
        def to(lat_peer, lon_peer):
            pltpu.make_async_remote_copy(
                source.at[lon_peer, :, lat_peer],
                landing.at[pl.ds(mine, OWN)],
                send.at[k],
                recv.at[k],
                device_id=(lat_peer, lon_peer),
                device_id_type=MESH,
            ).start()

        each_peer(lat, lon, to)
        return pltpu.make_async_copy(
            source.at[lon, :, lat], landing.at[pl.ds(mine, OWN)], load.at[k]
        )

    others = gate.at[pl.ds(0, CHANNELS - OWN)]

    def wait_for(semaphore):
        pltpu.make_async_copy(others, others, semaphore).wait()

    zonal_rows[...] = zonal[...].astype(F32)
    for j in range(OWN):
        row = jnp.concatenate(
            [zonal_rows[pl.ds(lon * OWN + j, 1), :], jnp.zeros((1, 256), F32)], axis=1
        )
        skew = pltpu.roll(
            jnp.broadcast_to(row, (COLS, 512)), 0, 1, stride=1, stride_axis=0
        )
        for d in range(3):
            block = skew[:, 256 - 128 * d : 384 - 128 * d]
            ahead[j, d * COLS : (d + 1) * COLS, :] = block.astype(BF16)
            back[j, (2 - d) * COLS : (3 - d) * COLS, :] = block.T.astype(BF16)
        line = meridional[pl.ds(lon * OWN + j, 1), :]
        turned = pltpu.roll(
            jnp.broadcast_to(line, (ROWS, COLS)), 0, 1, stride=1, stride_axis=0
        )
        lat_weights[j] = turned.astype(BF16)
    flip_cols, flip_rows = reversal(COLS), reversal(ROWS)

    signal_view = signal_in.reshape(LONS, OWN, ROWS, COLS)
    grad_view = grad_in.reshape(LONS, OWN, ROWS, COLS)
    conv_view = conv_src.reshape(LONS, OWN, ROWS, COLS)
    result_view = result_src.reshape(LONS, OWN, ROWS, COLS)

    wait_for(recv.at[0])
    backwards, flipped = [], []
    for j in range(OWN):
        blocks = [signal_view[b, j] for b in range(LONS)]
        filtered = dot(around_circle(blocks), ahead[j]).astype(BF16)
        wide = jnp.concatenate(
            [filtered[b * ROWS : (b + 1) * ROWS] for b in range(LONS)], axis=1
        )
        convolved = dot(lat_weights[j][:, :ROWS], wide, 0, 0).astype(BF16)
        for b in range(LONS):
            conv_view[b, j] = convolved[:, b * COLS : (b + 1) * COLS]
        flipped.append(dot(flip_rows, wide).astype(BF16))
    own_conv = give_back(conv_src, conv_in, 2)
    own_conv.start()
    for j in range(OWN):
        stack = jnp.concatenate([signal_view[b, j] for b in range(LONS)], axis=0)
        turned = dot(stack, flip_cols).astype(BF16)
        backwards.append([turned[b * ROWS : (b + 1) * ROWS] for b in range(LONS)])

    wait_for(recv.at[1])
    rounded = []
    for j in range(OWN):
        wide = jnp.concatenate([grad_view[b, j] for b in range(LONS)], axis=1)
        gradient = dot(lat_weights[j][:, :ROWS], wide).astype(BF16)
        blocks = [gradient[:, b * COLS : (b + 1) * COLS] for b in range(LONS)]
        rounded.append(jnp.concatenate(blocks, axis=0))
        result = dot(around_circle(blocks), back[j]).astype(BF16)
        for b in range(LONS):
            result_view[b, j] = result[b * ROWS : (b + 1) * ROWS]
    own_grad = give_back(result_src, grad_out, 3)
    own_grad.start()

    scale = 1.0 / 256.0
    for j in range(OWN):
        products = dot(around_circle(backwards[j]), rounded[j], 0, 0)
        side = jnp.concatenate(
            [products[2 * COLS :], products[COLS : 2 * COLS], products[:COLS], jnp.zeros((COLS, COLS), F32)],
            axis=1,
        )
        diagonals = pltpu.roll(side, 385, 1, stride=1, stride_axis=0)
        taps_src[pl.ds(j, 1), :256] = (
            jnp.sum(diagonals[:, :256], axis=0, keepdims=True) * scale
        )
        wide = jnp.concatenate([grad_view[b, j] for b in range(LONS)], axis=1)
        crossed = dot(flipped[j], wide, 1, 1)
        crossed = jnp.concatenate([crossed, jnp.zeros((ROWS, ROWS), F32)], axis=1)
        diagonals = pltpu.roll(crossed, 65, 1, stride=1, stride_axis=0)
        taps_src[pl.ds(j, 1), 256:] = jnp.sum(diagonals, axis=0, keepdims=True) * scale
    for step in range(1, LONS):
        pltpu.make_async_remote_copy(
            taps_src,
            taps_in.at[lon],
            send.at[4],
            recv.at[4],
            device_id=(lat, (lon + step) % LONS),
            device_id_type=MESH,
        ).start()
    taps_in[lon] = taps_src[...]

    seven = taps_in.at[pl.ds(0, LONS - 1)]
    pltpu.make_async_copy(seven, seven, recv.at[4]).wait()
    for b in range(LONS):
        for j in range(OWN):
            zonal_out[b * OWN + j : b * OWN + j + 1, :] = taps_in[b, j : j + 1, :256]
            meridional_out[b * OWN + j : b * OWN + j + 1, :] = taps_in[b, j : j + 1, 256:]

    own_conv.wait()
    wait_for(recv.at[2])
    convolved = conv_in.reshape(*flat)[...].astype(F32)
    mixed_out.reshape(*flat)[...] = (gate_flat[...].astype(F32) * convolved).astype(BF16)
    gate_out.reshape(*flat)[...] = (cotangent_flat[...].astype(F32) * convolved).astype(BF16)
    own_grad.wait()
    wait_for(recv.at[3])
    for k in range(4):
        wait_for(send.at[k])
    pltpu.make_async_copy(seven, seven, send.at[4]).wait()


def place_results(*refs):
    count = len(refs) // 2
    copies = [
        pltpu.make_async_copy(refs[k], refs[count + k], refs[-1].at[k])
        for k in range(count)
    ]
    for copy in copies:
        copy.start()
    for copy in copies:
        copy.wait()


def on_device(signal, gate, cotangent, zonal, meridional):
    field = (CHANNELS, 2, COLS)
    pencil = (LONS, OWN, LATS, 2, COLS)
    in_vmem = pl.BlockSpec(memory_space=pltpu.VMEM)
    in_hbm = pl.BlockSpec(memory_space=pltpu.HBM)
    results = [
        (field, BF16),
        (field, BF16),
        (field, BF16),
        ((GROUP, 256), F32),
        ((GROUP, 128), F32),
    ]
    inputs = [
        pltpu.with_memory_space_constraint(array, pltpu.HBM)
        for array in (signal, gate, cotangent, zonal, meridional)
    ]
    made = pl.pallas_call(
        mixer,
        out_shape=[pltpu.VMEM(*result) for result in results],
        in_specs=[in_hbm] * 5,
        out_specs=[in_vmem] * 5,
        scratch_shapes=[
            pltpu.VMEM(field, BF16),
            pltpu.VMEM(field, BF16),
            pltpu.VMEM((GROUP, 256), BF16),
            pltpu.VMEM((GROUP, 128), F32),
            pltpu.VMEM(field, BF16),
            pltpu.VMEM((GROUP, 256), F32),
            pltpu.VMEM(field, BF16),
            pltpu.VMEM(pencil, BF16),
            pltpu.VMEM(pencil, BF16),
            pltpu.VMEM(pencil, BF16),
            pltpu.VMEM(pencil, BF16),
            pltpu.VMEM((OWN, 3 * COLS, COLS), BF16),
            pltpu.VMEM((OWN, 3 * COLS, COLS), BF16),
            pltpu.VMEM((OWN, ROWS, COLS), BF16),
            pltpu.VMEM((8, 384), F32),
            pltpu.VMEM((LONS, 8, 384), F32),
            pltpu.SemaphoreType.DMA((5,)),
            pltpu.SemaphoreType.DMA((5,)),
            pltpu.SemaphoreType.DMA((5,)),
            pltpu.SemaphoreType.REGULAR,
        ],
        compiler_params=pltpu.CompilerParams(
            collective_id=0, has_side_effects=True, vmem_limit_bytes=VMEM_BYTES
        ),
        name="mixer",
    )(*inputs)
    return pl.pallas_call(
        place_results,
        out_shape=[pltpu.HBM(*result) for result in results],
        in_specs=[in_vmem] * 5,
        out_specs=[in_hbm] * 5,
        scratch_shapes=[pltpu.SemaphoreType.DMA((5,))],
        compiler_params=pltpu.CompilerParams(vmem_limit_bytes=VMEM_BYTES),
        name="place_results",
    )(*[pltpu.with_memory_space_constraint(array, pltpu.VMEM) for array in made])


def solution(mesh):
    fields = P(None, "lat", "lon")
    filters = P("lat", None)
    return jax.shard_map(
        on_device,
        mesh=mesh,
        in_specs=(fields, fields, fields, filters, filters),
        out_specs=(fields, fields, fields, filters, filters),
        check_vma=False,
    )
```

```python
import jax
import jax.numpy as jnp
from jax import lax
from jax.experimental import pallas as pl
from jax.experimental.pallas import tpu as pltpu
from jax.sharding import PartitionSpec as P

MESH = pl.DeviceIdType.MESH
BF16 = jnp.bfloat16
F32 = jnp.float32
LATS, LONS = 32, 8
CHANNELS = 768
GROUP = 24
VMEM_BYTES = 32 * 1024 * 1024
OWN = 3
ROWS = 64
COLS = 128
Z_STEPS = (4, 3, 5, 2, 6, 1, 7)


def dot(a, b, a_dim=1, b_dim=0):
    return lax.dot_general(
        a, b, (((a_dim,), (b_dim,)), ((), ())), preferred_element_type=F32
    )


def place():
    lat, lon = lax.axis_index("lat"), lax.axis_index("lon")
    return lat, lon


def each_peer(lat, lon, visit, first=True, rest=True):
    if first:
        column, plane = neighbours(lat, lon)
        for peer in column + plane:
            visit(*peer)
    if not rest:
        return
    y_lo, z, core = lat // 16, (lat // 2) % 8, lat % 2
    x, y = lon // 2, (lon % 2) * 2 + y_lo

    def toward(i, steps, same_core):
        x_peer, y_peer = (x + i % 4) % 4, (y + i // 4) % 4
        core_peer = core if same_core else 1 - core
        lat_base = (y_peer % 2) * 16 + core_peer
        for step in steps:
            visit(lat_base + ((z + step) % 8) * 2, x_peer * 2 + y_peer // 2)

    for steps in (Z_STEPS, (0,)):

        def around(i, carry):
            if steps is Z_STEPS:
                toward(i, steps, True)
            toward(i, steps, False)
            return carry

        lax.fori_loop(1, 16, around, 0)


def neighbours(lat, lon):
    y_lo, z, core = lat // 16, (lat // 2) % 8, lat % 2
    x, y = lon // 2, (lon % 2) * 2 + y_lo
    column = [
        (y_lo * 16 + ((z + step) % 8) * 2 + (core + other) % 2, lon)
        for other in (1, 0)
        for step in Z_STEPS + (0,)
        if step or other
    ]
    plane = []
    for y_step in (1, 3, 2, 0):
        for x_step in (1, 3, 2, 0):
            if x_step or y_step:
                x_peer, y_peer = (x + x_step) % 4, (y + y_step) % 4
                plane.append(
                    ((y_peer % 2) * 16 + z * 2 + core, x_peer * 2 + y_peer // 2)
                )
    return column, plane


def reversal(size):
    rows = lax.broadcasted_iota(jnp.int32, (size, size), 0)
    cols = lax.broadcasted_iota(jnp.int32, (size, size), 1)
    return jnp.where(rows + cols == size - 1, 1.0, 0.0).astype(BF16)


def around_circle(blocks):
    return jnp.concatenate(
        [
            jnp.concatenate([blocks[(b + d - 1) % LONS] for d in range(3)], axis=1)
            for b in range(LONS)
        ],
        axis=0,
    )


def mixer(
    signal,
    gate_hbm,
    cotangent_hbm,
    zonal_hbm,
    meridional_hbm,
    mixed_out,
    gate_out,
    grad_out,
    zonal_out,
    meridional_out,
    gate,
    cotangent,
    zonal,
    meridional,
    conv_in,
    zonal_rows,
    grad_src,
    signal_in,
    grad_in,
    conv_src,
    result_src,
    ahead,
    back,
    lat_weights,
    taps_src,
    taps_in,
    send,
    recv,
    load,
    ready,
):
    lat, lon = place()
    mine = lat * GROUP + lon * OWN
    column, plane = neighbours(lat, lon)
    barrier = pltpu.get_barrier_semaphore()
    for peer in column + plane:
        pl.semaphore_signal(barrier, inc=1, device_id=peer, device_id_type=MESH)

    loads = [
        pltpu.make_async_copy(source, target, load.at[k])
        for k, (source, target) in enumerate(
            (
                (gate_hbm, gate),
                (cotangent_hbm, cotangent),
                (signal.at[pl.ds(mine, OWN)], signal_in.at[lon, :, lat]),
                (zonal_hbm, zonal),
                (meridional_hbm, meridional),
            )
        )
    ]
    for copy in loads:
        copy.start()

    pl.semaphore_wait(barrier, len(column) + len(plane))
    for peer in plane:
        pl.semaphore_signal(ready, inc=1, device_id=peer, device_id_type=MESH)

    def spread(source, landing, k, **which):
        def to(lat_peer, lon_peer):
            pltpu.make_async_remote_copy(
                source.at[pl.ds(lat_peer * GROUP + lon_peer * OWN, OWN)],
                landing.at[lon, :, lat],
                send.at[k],
                recv.at[k],
                device_id=(lat_peer, lon_peer),
                device_id_type=MESH,
            ).start()

        each_peer(lat, lon, to, **which)

    spread(signal, signal_in, 0, rest=False)
    for copy in loads:
        copy.wait()
    flat = (CHANNELS * 2, COLS)
    gate_flat, cotangent_flat = gate.reshape(*flat), cotangent.reshape(*flat)
    product = gate_flat[...].astype(F32) * cotangent_flat[...].astype(F32)
    grad_src.reshape(*flat)[...] = product.astype(BF16)
    spread(grad_src, grad_in, 1, rest=False)
    grad_in[lon, :, lat] = grad_src[pl.ds(mine, OWN)]

    pl.semaphore_wait(ready, len(plane))
    spread(signal, signal_in, 0, first=False)

    def give_back(source, landing, k, corner_first=False):
        def to(lat_peer, lon_peer):
            pltpu.make_async_remote_copy(
                source.at[lon_peer, :, lat_peer],
                landing.at[pl.ds(mine, OWN)],
                send.at[k],
                recv.at[k],
                device_id=(lat_peer, lon_peer),
                device_id_type=MESH,
            ).start()

        if corner_first:
            for corner in range(2):

                @pl.when((lat != corner) | (lon != 0))
                def _():
                    to(corner, 0)

        def unless_corner(lat_peer, lon_peer):
            @pl.when((lat_peer > 1) | (lon_peer > 0))
            def _():
                to(lat_peer, lon_peer)

        each_peer(lat, lon, unless_corner if corner_first else to)
        return pltpu.make_async_copy(
            source.at[lon, :, lat], landing.at[pl.ds(mine, OWN)], load.at[k]
        )

    others = gate.at[pl.ds(0, CHANNELS - OWN)]

    def wait_for(semaphore):
        pltpu.make_async_copy(others, others, semaphore).wait()

    zonal_rows[...] = zonal[...].astype(F32)
    for j in range(OWN):
        row = jnp.concatenate(
            [zonal_rows[pl.ds(lon * OWN + j, 1), :], jnp.zeros((1, 256), F32)], axis=1
        )
        skew = pltpu.roll(
            jnp.broadcast_to(row, (COLS, 512)), 0, 1, stride=1, stride_axis=0
        )
        for d in range(3):
            block = skew[:, 256 - 128 * d : 384 - 128 * d]
            ahead[j, d * COLS : (d + 1) * COLS, :] = block.astype(BF16)
            back[j, (2 - d) * COLS : (3 - d) * COLS, :] = block.T.astype(BF16)
        line = meridional[pl.ds(lon * OWN + j, 1), :]
        turned = pltpu.roll(
            jnp.broadcast_to(line, (ROWS, COLS)), 0, 1, stride=1, stride_axis=0
        )
        lat_weights[j] = turned.astype(BF16)
    flip_cols, flip_rows = reversal(COLS), reversal(ROWS)

    spread(grad_src, grad_in, 1, first=False)

    signal_view = signal_in.reshape(LONS, OWN, ROWS, COLS)
    grad_view = grad_in.reshape(LONS, OWN, ROWS, COLS)
    conv_view = conv_src.reshape(LONS, OWN, ROWS, COLS)
    result_view = result_src.reshape(LONS, OWN, ROWS, COLS)

    wait_for(recv.at[0])
    backwards, flipped = [], []
    for j in range(OWN):
        blocks = [signal_view[b, j] for b in range(LONS)]
        filtered = dot(around_circle(blocks), ahead[j]).astype(BF16)
        wide = jnp.concatenate(
            [filtered[b * ROWS : (b + 1) * ROWS] for b in range(LONS)], axis=1
        )
        convolved = dot(lat_weights[j][:, :ROWS], wide, 0, 0).astype(BF16)
        for b in range(LONS):
            conv_view[b, j] = convolved[:, b * COLS : (b + 1) * COLS]
        flipped.append(dot(flip_rows, wide).astype(BF16))
    own_conv = give_back(conv_src, conv_in, 2)
    own_conv.start()
    for j in range(OWN):
        stack = jnp.concatenate([signal_view[b, j] for b in range(LONS)], axis=0)
        turned = dot(stack, flip_cols).astype(BF16)
        backwards.append([turned[b * ROWS : (b + 1) * ROWS] for b in range(LONS)])

    wait_for(recv.at[1])
    rounded = []
    for j in range(OWN):
        wide = jnp.concatenate([grad_view[b, j] for b in range(LONS)], axis=1)
        gradient = dot(lat_weights[j][:, :ROWS], wide).astype(BF16)
        blocks = [gradient[:, b * COLS : (b + 1) * COLS] for b in range(LONS)]
        rounded.append(jnp.concatenate(blocks, axis=0))
        result = dot(around_circle(blocks), back[j]).astype(BF16)
        for b in range(LONS):
            result_view[b, j] = result[b * ROWS : (b + 1) * ROWS]
    own_grad = give_back(result_src, grad_out, 3, corner_first=True)
    own_grad.start()

    scale = 1.0 / 256.0
    for j in range(OWN):
        products = dot(around_circle(backwards[j]), rounded[j], 0, 0)
        side = jnp.concatenate(
            [products[2 * COLS :], products[COLS : 2 * COLS], products[:COLS], jnp.zeros((COLS, COLS), F32)],
            axis=1,
        )
        diagonals = pltpu.roll(side, 385, 1, stride=1, stride_axis=0)
        taps_src[pl.ds(j, 1), :256] = (
            jnp.sum(diagonals[:, :256], axis=0, keepdims=True) * scale
        )
        wide = jnp.concatenate([grad_view[b, j] for b in range(LONS)], axis=1)
        crossed = dot(flipped[j], wide, 1, 1)
        crossed = jnp.concatenate([crossed, jnp.zeros((ROWS, ROWS), F32)], axis=1)
        diagonals = pltpu.roll(crossed, 65, 1, stride=1, stride_axis=0)
        taps_src[pl.ds(j, 1), 256:] = jnp.sum(diagonals, axis=0, keepdims=True) * scale
    for step in range(1, LONS):
        pltpu.make_async_remote_copy(
            taps_src,
            taps_in.at[lon],
            send.at[4],
            recv.at[4],
            device_id=(lat, (lon + step) % LONS),
            device_id_type=MESH,
        ).start()
    taps_in[lon] = taps_src[...]

    seven = taps_in.at[pl.ds(0, LONS - 1)]
    pltpu.make_async_copy(seven, seven, recv.at[4]).wait()
    for b in range(LONS):
        for j in range(OWN):
            zonal_out[b * OWN + j : b * OWN + j + 1, :] = taps_in[b, j : j + 1, :256]
            meridional_out[b * OWN + j : b * OWN + j + 1, :] = taps_in[b, j : j + 1, 256:]

    own_conv.wait()
    wait_for(recv.at[2])
    convolved = conv_in.reshape(*flat)[...].astype(F32)
    mixed_out.reshape(*flat)[...] = (gate_flat[...].astype(F32) * convolved).astype(BF16)
    gate_out.reshape(*flat)[...] = (cotangent_flat[...].astype(F32) * convolved).astype(BF16)
    own_grad.wait()
    wait_for(recv.at[3])
    for k in range(4):
        wait_for(send.at[k])
    pltpu.make_async_copy(seven, seven, send.at[4]).wait()


def place_results(*refs):
    count = len(refs) // 2
    copies = [
        pltpu.make_async_copy(refs[k], refs[count + k], refs[-1].at[k])
        for k in range(count)
    ]
    for copy in copies:
        copy.start()
    for copy in copies:
        copy.wait()


def on_device(signal, gate, cotangent, zonal, meridional):
    field = (CHANNELS, 2, COLS)
    pencil = (LONS, OWN, LATS, 2, COLS)
    in_vmem = pl.BlockSpec(memory_space=pltpu.VMEM)
    in_hbm = pl.BlockSpec(memory_space=pltpu.HBM)
    results = [
        (field, BF16),
        (field, BF16),
        (field, BF16),
        ((GROUP, 256), F32),
        ((GROUP, 128), F32),
    ]
    inputs = [
        pltpu.with_memory_space_constraint(array, pltpu.HBM)
        for array in (signal, gate, cotangent, zonal, meridional)
    ]
    made = pl.pallas_call(
        mixer,
        out_shape=[pltpu.VMEM(*result) for result in results],
        in_specs=[in_hbm] * 5,
        out_specs=[in_vmem] * 5,
        scratch_shapes=[
            pltpu.VMEM(field, BF16),
            pltpu.VMEM(field, BF16),
            pltpu.VMEM((GROUP, 256), BF16),
            pltpu.VMEM((GROUP, 128), F32),
            pltpu.VMEM(field, BF16),
            pltpu.VMEM((GROUP, 256), F32),
            pltpu.VMEM(field, BF16),
            pltpu.VMEM(pencil, BF16),
            pltpu.VMEM(pencil, BF16),
            pltpu.VMEM(pencil, BF16),
            pltpu.VMEM(pencil, BF16),
            pltpu.VMEM((OWN, 3 * COLS, COLS), BF16),
            pltpu.VMEM((OWN, 3 * COLS, COLS), BF16),
            pltpu.VMEM((OWN, ROWS, COLS), BF16),
            pltpu.VMEM((8, 384), F32),
            pltpu.VMEM((LONS, 8, 384), F32),
            pltpu.SemaphoreType.DMA((5,)),
            pltpu.SemaphoreType.DMA((5,)),
            pltpu.SemaphoreType.DMA((5,)),
            pltpu.SemaphoreType.REGULAR,
        ],
        compiler_params=pltpu.CompilerParams(
            collective_id=0, has_side_effects=True, vmem_limit_bytes=VMEM_BYTES
        ),
        name="mixer",
    )(*inputs)
    return pl.pallas_call(
        place_results,
        out_shape=[pltpu.HBM(*result) for result in results],
        in_specs=[in_vmem] * 5,
        out_specs=[in_hbm] * 5,
        scratch_shapes=[pltpu.SemaphoreType.DMA((5,))],
        compiler_params=pltpu.CompilerParams(vmem_limit_bytes=VMEM_BYTES),
        name="place_results",
    )(*[pltpu.with_memory_space_constraint(array, pltpu.VMEM) for array in made])


def solution(mesh):
    fields = P(None, "lat", "lon")
    filters = P("lat", None)
    return jax.shard_map(
        on_device,
        mesh=mesh,
        in_specs=(fields, fields, fields, filters, filters),
        out_specs=(fields, fields, fields, filters, filters),
        check_vma=False,
    )
```

```python
import jax
import jax.numpy as jnp
from jax import lax
from jax.experimental import pallas as pl
from jax.experimental.pallas import tpu as pltpu
from jax.sharding import PartitionSpec as P

MESH = pl.DeviceIdType.MESH
BF16 = jnp.bfloat16
F32 = jnp.float32
LATS, LONS = 32, 8
CHANNELS = 768
GROUP = 24
VMEM_BYTES = 32 * 1024 * 1024
OWN = 3
ROWS = 64
COLS = 128
Z_STEPS = (4, 3, 5, 2, 6, 1, 7)


PLANE_STEPS = (
    (2, 2), (1, 2), (3, 2), (2, 1), (2, 3), (1, 1), (3, 3), (1, 3),
    (3, 1), (2, 0), (0, 2), (1, 0), (3, 0), (0, 1), (0, 3),
)


def dot(a, b, a_dim=1, b_dim=0):
    return lax.dot_general(
        a, b, (((a_dim,), (b_dim,)), ((), ())), preferred_element_type=F32
    )


def place():
    lat, lon = lax.axis_index("lat"), lax.axis_index("lon")
    return lat, lon


def each_peer(lat, lon, visit, first=True, rest=True):
    if first:
        column, plane = neighbours(lat, lon)
        for peer in column + plane:
            visit(*peer)
    if not rest:
        return
    y_lo, z, core = lat // 16, (lat // 2) % 8, lat % 2
    x, y = lon // 2, (lon % 2) * 2 + y_lo

    def toward(x_step, y_step, steps, same_core):
        x_peer, y_peer = (x + x_step) % 4, (y + y_step) % 4
        core_peer = core if same_core else 1 - core
        lat_base = (y_peer % 2) * 16 + core_peer
        for step in steps:
            visit(lat_base + ((z + step) % 8) * 2, x_peer * 2 + y_peer // 2)

    for steps in (Z_STEPS, (0,)):

        def around(i, digits):
            x_digits, y_digits = digits
            x_step, y_step = x_digits % 4, y_digits % 4
            if steps is Z_STEPS:
                toward(x_step, y_step, steps, True)
            toward(x_step, y_step, steps, False)
            return x_digits // 4, y_digits // 4

        digits = [
            jnp.int32(sum(step[axis] * 4**i for i, step in enumerate(PLANE_STEPS)))
            for axis in range(2)
        ]
        lax.fori_loop(0, len(PLANE_STEPS), around, tuple(digits))


def neighbours(lat, lon):
    y_lo, z, core = lat // 16, (lat // 2) % 8, lat % 2
    x, y = lon // 2, (lon % 2) * 2 + y_lo
    column = [
        (y_lo * 16 + ((z + step) % 8) * 2 + (core + other) % 2, lon)
        for other in (1, 0)
        for step in Z_STEPS + (0,)
        if step or other
    ]
    plane = []
    for y_step in (1, 3, 2, 0):
        for x_step in (1, 3, 2, 0):
            if x_step or y_step:
                x_peer, y_peer = (x + x_step) % 4, (y + y_step) % 4
                plane.append(
                    ((y_peer % 2) * 16 + z * 2 + core, x_peer * 2 + y_peer // 2)
                )
    return column, plane


def reversal(size):
    rows = lax.broadcasted_iota(jnp.int32, (size, size), 0)
    cols = lax.broadcasted_iota(jnp.int32, (size, size), 1)
    return jnp.where(rows + cols == size - 1, 1.0, 0.0).astype(BF16)


def around_circle(blocks):
    return jnp.concatenate(
        [
            jnp.concatenate([blocks[(b + d - 1) % LONS] for d in range(3)], axis=1)
            for b in range(LONS)
        ],
        axis=0,
    )


def mixer(
    signal,
    gate_hbm,
    cotangent_hbm,
    zonal_hbm,
    meridional_hbm,
    mixed_out,
    gate_out,
    grad_out,
    zonal_out,
    meridional_out,
    gate,
    cotangent,
    zonal,
    meridional,
    conv_in,
    zonal_rows,
    grad_src,
    signal_in,
    grad_in,
    conv_src,
    result_src,
    ahead,
    back,
    lat_weights,
    taps_src,
    taps_in,
    send,
    recv,
    load,
    ready,
):
    lat, lon = place()
    mine = lat * GROUP + lon * OWN
    column, plane = neighbours(lat, lon)
    barrier = pltpu.get_barrier_semaphore()
    for peer in column + plane:
        pl.semaphore_signal(barrier, inc=1, device_id=peer, device_id_type=MESH)

    loads = [
        pltpu.make_async_copy(source, target, load.at[k])
        for k, (source, target) in enumerate(
            (
                (gate_hbm, gate),
                (cotangent_hbm, cotangent),
                (signal.at[pl.ds(mine, OWN)], signal_in.at[lon, :, lat]),
                (zonal_hbm, zonal),
                (meridional_hbm, meridional),
            )
        )
    ]
    for copy in loads:
        copy.start()

    pl.semaphore_wait(barrier, len(column) + len(plane))
    for peer in plane:
        pl.semaphore_signal(ready, inc=1, device_id=peer, device_id_type=MESH)

    def spread(source, landing, k, **which):
        def to(lat_peer, lon_peer):
            pltpu.make_async_remote_copy(
                source.at[pl.ds(lat_peer * GROUP + lon_peer * OWN, OWN)],
                landing.at[lon, :, lat],
                send.at[k],
                recv.at[k],
                device_id=(lat_peer, lon_peer),
                device_id_type=MESH,
            ).start()

        each_peer(lat, lon, to, **which)

    spread(signal, signal_in, 0, rest=False)
    for copy in loads:
        copy.wait()
    flat = (CHANNELS * 2, COLS)
    gate_flat, cotangent_flat = gate.reshape(*flat), cotangent.reshape(*flat)
    product = gate_flat[...].astype(F32) * cotangent_flat[...].astype(F32)
    grad_src.reshape(*flat)[...] = product.astype(BF16)
    spread(grad_src, grad_in, 1, rest=False)
    grad_in[lon, :, lat] = grad_src[pl.ds(mine, OWN)]

    pl.semaphore_wait(ready, len(plane))
    spread(signal, signal_in, 0, first=False)

    def give_back(source, landing, k, corner_first=False):
        def to(lat_peer, lon_peer):
            pltpu.make_async_remote_copy(
                source.at[lon_peer, :, lat_peer],
                landing.at[pl.ds(mine, OWN)],
                send.at[k],
                recv.at[k],
                device_id=(lat_peer, lon_peer),
                device_id_type=MESH,
            ).start()

        if corner_first:
            for corner in range(2):

                @pl.when((lat != corner) | (lon != 0))
                def _():
                    to(corner, 0)

        def unless_corner(lat_peer, lon_peer):
            @pl.when((lat_peer > 1) | (lon_peer > 0))
            def _():
                to(lat_peer, lon_peer)

        visit = unless_corner if corner_first else to
        each_peer(lat, lon, visit, first=False)
        each_peer(lat, lon, visit, rest=False)
        return pltpu.make_async_copy(
            source.at[lon, :, lat], landing.at[pl.ds(mine, OWN)], load.at[k]
        )

    others = gate.at[pl.ds(0, CHANNELS - OWN)]

    def wait_for(semaphore):
        pltpu.make_async_copy(others, others, semaphore).wait()

    zonal_rows[...] = zonal[...].astype(F32)
    for j in range(OWN):
        row = jnp.concatenate(
            [zonal_rows[pl.ds(lon * OWN + j, 1), :], jnp.zeros((1, 256), F32)], axis=1
        )
        skew = pltpu.roll(
            jnp.broadcast_to(row, (COLS, 512)), 0, 1, stride=1, stride_axis=0
        )
        for d in range(3):
            block = skew[:, 256 - 128 * d : 384 - 128 * d]
            ahead[j, d * COLS : (d + 1) * COLS, :] = block.astype(BF16)
            back[j, (2 - d) * COLS : (3 - d) * COLS, :] = block.T.astype(BF16)
        line = meridional[pl.ds(lon * OWN + j, 1), :]
        turned = pltpu.roll(
            jnp.broadcast_to(line, (ROWS, COLS)), 0, 1, stride=1, stride_axis=0
        )
        lat_weights[j] = turned.astype(BF16)
    flip_cols, flip_rows = reversal(COLS), reversal(ROWS)

    spread(grad_src, grad_in, 1, first=False)

    signal_view = signal_in.reshape(LONS, OWN, ROWS, COLS)
    grad_view = grad_in.reshape(LONS, OWN, ROWS, COLS)
    conv_view = conv_src.reshape(LONS, OWN, ROWS, COLS)
    result_view = result_src.reshape(LONS, OWN, ROWS, COLS)

    wait_for(recv.at[0])
    backwards, flipped = [], []
    for j in range(OWN):
        blocks = [signal_view[b, j] for b in range(LONS)]
        filtered = dot(around_circle(blocks), ahead[j]).astype(BF16)
        wide = jnp.concatenate(
            [filtered[b * ROWS : (b + 1) * ROWS] for b in range(LONS)], axis=1
        )
        convolved = dot(lat_weights[j][:, :ROWS], wide, 0, 0).astype(BF16)
        for b in range(LONS):
            conv_view[b, j] = convolved[:, b * COLS : (b + 1) * COLS]
        flipped.append(dot(flip_rows, wide).astype(BF16))
    own_conv = give_back(conv_src, conv_in, 2)
    own_conv.start()
    for j in range(OWN):
        stack = jnp.concatenate([signal_view[b, j] for b in range(LONS)], axis=0)
        turned = dot(stack, flip_cols).astype(BF16)
        backwards.append([turned[b * ROWS : (b + 1) * ROWS] for b in range(LONS)])

    wait_for(recv.at[1])
    rounded = []
    for j in range(OWN):
        wide = jnp.concatenate([grad_view[b, j] for b in range(LONS)], axis=1)
        gradient = dot(lat_weights[j][:, :ROWS], wide).astype(BF16)
        blocks = [gradient[:, b * COLS : (b + 1) * COLS] for b in range(LONS)]
        rounded.append(jnp.concatenate(blocks, axis=0))
        result = dot(around_circle(blocks), back[j]).astype(BF16)
        for b in range(LONS):
            result_view[b, j] = result[b * ROWS : (b + 1) * ROWS]
    own_grad = give_back(result_src, grad_out, 3, corner_first=True)
    own_grad.start()

    scale = 1.0 / 256.0
    for j in range(OWN):
        products = dot(around_circle(backwards[j]), rounded[j], 0, 0)
        side = jnp.concatenate(
            [products[2 * COLS :], products[COLS : 2 * COLS], products[:COLS], jnp.zeros((COLS, COLS), F32)],
            axis=1,
        )
        diagonals = pltpu.roll(side, 385, 1, stride=1, stride_axis=0)
        taps_src[pl.ds(j, 1), :256] = (
            jnp.sum(diagonals[:, :256], axis=0, keepdims=True) * scale
        )
        wide = jnp.concatenate([grad_view[b, j] for b in range(LONS)], axis=1)
        crossed = dot(flipped[j], wide, 1, 1)
        crossed = jnp.concatenate([crossed, jnp.zeros((ROWS, ROWS), F32)], axis=1)
        diagonals = pltpu.roll(crossed, 65, 1, stride=1, stride_axis=0)
        taps_src[pl.ds(j, 1), 256:] = jnp.sum(diagonals, axis=0, keepdims=True) * scale
    for step in range(1, LONS):
        pltpu.make_async_remote_copy(
            taps_src,
            taps_in.at[lon],
            send.at[4],
            recv.at[4],
            device_id=(lat, (lon + step) % LONS),
            device_id_type=MESH,
        ).start()
    taps_in[lon] = taps_src[...]

    seven = taps_in.at[pl.ds(0, LONS - 1)]
    pltpu.make_async_copy(seven, seven, recv.at[4]).wait()
    for b in range(LONS):
        for j in range(OWN):
            zonal_out[b * OWN + j : b * OWN + j + 1, :] = taps_in[b, j : j + 1, :256]
            meridional_out[b * OWN + j : b * OWN + j + 1, :] = taps_in[b, j : j + 1, 256:]

    own_conv.wait()
    wait_for(recv.at[2])
    convolved = conv_in.reshape(*flat)[...].astype(F32)
    mixed_out.reshape(*flat)[...] = (gate_flat[...].astype(F32) * convolved).astype(BF16)
    gate_out.reshape(*flat)[...] = (cotangent_flat[...].astype(F32) * convolved).astype(BF16)
    own_grad.wait()
    wait_for(recv.at[3])
    for k in range(4):
        wait_for(send.at[k])
    pltpu.make_async_copy(seven, seven, send.at[4]).wait()


def place_results(*refs):
    count = len(refs) // 2
    copies = [
        pltpu.make_async_copy(refs[k], refs[count + k], refs[-1].at[k])
        for k in range(count)
    ]
    for copy in copies:
        copy.start()
    for copy in copies:
        copy.wait()


def on_device(signal, gate, cotangent, zonal, meridional):
    field = (CHANNELS, 2, COLS)
    pencil = (LONS, OWN, LATS, 2, COLS)
    in_vmem = pl.BlockSpec(memory_space=pltpu.VMEM)
    in_hbm = pl.BlockSpec(memory_space=pltpu.HBM)
    results = [
        (field, BF16),
        (field, BF16),
        (field, BF16),
        ((GROUP, 256), F32),
        ((GROUP, 128), F32),
    ]
    inputs = [
        pltpu.with_memory_space_constraint(array, pltpu.HBM)
        for array in (signal, gate, cotangent, zonal, meridional)
    ]
    made = pl.pallas_call(
        mixer,
        out_shape=[pltpu.VMEM(*result) for result in results],
        in_specs=[in_hbm] * 5,
        out_specs=[in_vmem] * 5,
        scratch_shapes=[
            pltpu.VMEM(field, BF16),
            pltpu.VMEM(field, BF16),
            pltpu.VMEM((GROUP, 256), BF16),
            pltpu.VMEM((GROUP, 128), F32),
            pltpu.VMEM(field, BF16),
            pltpu.VMEM((GROUP, 256), F32),
            pltpu.VMEM(field, BF16),
            pltpu.VMEM(pencil, BF16),
            pltpu.VMEM(pencil, BF16),
            pltpu.VMEM(pencil, BF16),
            pltpu.VMEM(pencil, BF16),
            pltpu.VMEM((OWN, 3 * COLS, COLS), BF16),
            pltpu.VMEM((OWN, 3 * COLS, COLS), BF16),
            pltpu.VMEM((OWN, ROWS, COLS), BF16),
            pltpu.VMEM((8, 384), F32),
            pltpu.VMEM((LONS, 8, 384), F32),
            pltpu.SemaphoreType.DMA((5,)),
            pltpu.SemaphoreType.DMA((5,)),
            pltpu.SemaphoreType.DMA((5,)),
            pltpu.SemaphoreType.REGULAR,
        ],
        compiler_params=pltpu.CompilerParams(
            collective_id=0, has_side_effects=True, vmem_limit_bytes=VMEM_BYTES
        ),
        name="mixer",
    )(*inputs)
    return pl.pallas_call(
        place_results,
        out_shape=[pltpu.HBM(*result) for result in results],
        in_specs=[in_vmem] * 5,
        out_specs=[in_hbm] * 5,
        scratch_shapes=[pltpu.SemaphoreType.DMA((5,))],
        compiler_params=pltpu.CompilerParams(vmem_limit_bytes=VMEM_BYTES),
        name="place_results",
    )(*[pltpu.with_memory_space_constraint(array, pltpu.VMEM) for array in made])


def solution(mesh):
    fields = P(None, "lat", "lon")
    filters = P("lat", None)
    return jax.shard_map(
        on_device,
        mesh=mesh,
        in_specs=(fields, fields, fields, filters, filters),
        out_specs=(fields, fields, fields, filters, filters),
        check_vma=False,
    )
```

```python
import jax
import jax.numpy as jnp
from jax import lax
from jax.experimental import pallas as pl
from jax.experimental.pallas import tpu as pltpu
from jax.sharding import PartitionSpec as P

MESH = pl.DeviceIdType.MESH
BF16 = jnp.bfloat16
F32 = jnp.float32
LATS, LONS = 32, 8
CHANNELS = 768
GROUP = 24
VMEM_BYTES = 32 * 1024 * 1024
OWN = 3
ROWS = 64
COLS = 128
Z_STEPS = (4, 3, 5, 2, 6, 1, 7)


PLANE_STEPS = (
    (2, 2), (1, 2), (3, 2), (2, 1), (2, 3), (1, 1), (3, 3), (1, 3),
    (3, 1), (2, 0), (0, 2), (1, 0), (3, 0), (0, 1), (0, 3),
)


def dot(a, b, a_dim=1, b_dim=0):
    return lax.dot_general(
        a, b, (((a_dim,), (b_dim,)), ((), ())), preferred_element_type=F32
    )


def place():
    lat, lon = lax.axis_index("lat"), lax.axis_index("lon")
    return lat, lon


def each_peer(lat, lon, visit, first=True, rest=True):
    if first:
        column, plane = neighbours(lat, lon)
        for peer in column + plane:
            visit(*peer)
    if not rest:
        return
    y_lo, z, core = lat // 16, (lat // 2) % 8, lat % 2
    x, y = lon // 2, (lon % 2) * 2 + y_lo

    def toward(x_step, y_step, steps, same_core):
        x_peer, y_peer = (x + x_step) % 4, (y + y_step) % 4
        core_peer = core if same_core else 1 - core
        lat_base = (y_peer % 2) * 16 + core_peer
        for step in steps:
            visit(lat_base + ((z + step + core * (8 - 2 * step)) % 8) * 2, x_peer * 2 + y_peer // 2)

    for steps in (Z_STEPS, (0,)):

        def around(i, digits):
            x_digits, y_digits = digits
            x_step, y_step = x_digits % 4, y_digits % 4
            if steps is Z_STEPS:
                toward(x_step, y_step, steps, True)
            toward(x_step, y_step, steps, False)
            return x_digits // 4, y_digits // 4

        digits = [
            jnp.int32(sum(step[axis] * 4**i for i, step in enumerate(PLANE_STEPS)))
            for axis in range(2)
        ]
        lax.fori_loop(0, len(PLANE_STEPS), around, tuple(digits))


def neighbours(lat, lon):
    y_lo, z, core = lat // 16, (lat // 2) % 8, lat % 2
    x, y = lon // 2, (lon % 2) * 2 + y_lo
    column = [
        (y_lo * 16 + ((z + step) % 8) * 2 + (core + other) % 2, lon)
        for other in (1, 0)
        for step in Z_STEPS + (0,)
        if step or other
    ]
    plane = []
    for y_step in (1, 3, 2, 0):
        for x_step in (1, 3, 2, 0):
            if x_step or y_step:
                x_peer, y_peer = (x + x_step) % 4, (y + y_step) % 4
                plane.append(
                    ((y_peer % 2) * 16 + z * 2 + core, x_peer * 2 + y_peer // 2)
                )
    return column, plane


def reversal(size):
    rows = lax.broadcasted_iota(jnp.int32, (size, size), 0)
    cols = lax.broadcasted_iota(jnp.int32, (size, size), 1)
    return jnp.where(rows + cols == size - 1, 1.0, 0.0).astype(BF16)


def around_circle(blocks):
    return jnp.concatenate(
        [
            jnp.concatenate([blocks[(b + d - 1) % LONS] for d in range(3)], axis=1)
            for b in range(LONS)
        ],
        axis=0,
    )


def mixer(
    signal,
    gate_hbm,
    cotangent_hbm,
    zonal_hbm,
    meridional_hbm,
    mixed_out,
    gate_out,
    grad_out,
    zonal_out,
    meridional_out,
    gate,
    cotangent,
    zonal,
    meridional,
    conv_in,
    zonal_rows,
    grad_src,
    signal_in,
    grad_in,
    conv_src,
    result_src,
    ahead,
    back,
    lat_weights,
    taps_src,
    taps_in,
    send,
    recv,
    load,
    ready,
):
    lat, lon = place()
    mine = lat * GROUP + lon * OWN
    column, plane = neighbours(lat, lon)
    barrier = pltpu.get_barrier_semaphore()
    for peer in column + plane:
        pl.semaphore_signal(barrier, inc=1, device_id=peer, device_id_type=MESH)

    loads = [
        pltpu.make_async_copy(source, target, load.at[k])
        for k, (source, target) in enumerate(
            (
                (gate_hbm, gate),
                (cotangent_hbm, cotangent),
                (signal.at[pl.ds(mine, OWN)], signal_in.at[lon, :, lat]),
                (zonal_hbm, zonal),
                (meridional_hbm, meridional),
            )
        )
    ]
    for copy in loads:
        copy.start()

    pl.semaphore_wait(barrier, len(column) + len(plane))
    for peer in plane:
        pl.semaphore_signal(ready, inc=1, device_id=peer, device_id_type=MESH)

    def spread(source, landing, k, **which):
        def to(lat_peer, lon_peer):
            pltpu.make_async_remote_copy(
                source.at[pl.ds(lat_peer * GROUP + lon_peer * OWN, OWN)],
                landing.at[lon, :, lat],
                send.at[k],
                recv.at[k],
                device_id=(lat_peer, lon_peer),
                device_id_type=MESH,
            ).start()

        each_peer(lat, lon, to, **which)

    spread(signal, signal_in, 0, rest=False)
    for copy in loads:
        copy.wait()
    flat = (CHANNELS * 2, COLS)
    gate_flat, cotangent_flat = gate.reshape(*flat), cotangent.reshape(*flat)
    product = gate_flat[...].astype(F32) * cotangent_flat[...].astype(F32)
    grad_src.reshape(*flat)[...] = product.astype(BF16)
    spread(grad_src, grad_in, 1, rest=False)
    grad_in[lon, :, lat] = grad_src[pl.ds(mine, OWN)]

    pl.semaphore_wait(ready, len(plane))
    spread(signal, signal_in, 0, first=False)

    def give_back(source, landing, k, corner_first=False):
        def to(lat_peer, lon_peer):
            pltpu.make_async_remote_copy(
                source.at[lon_peer, :, lat_peer],
                landing.at[pl.ds(mine, OWN)],
                send.at[k],
                recv.at[k],
                device_id=(lat_peer, lon_peer),
                device_id_type=MESH,
            ).start()

        if corner_first:
            for corner in range(2):

                @pl.when((lat != corner) | (lon != 0))
                def _():
                    to(corner, 0)

        def unless_corner(lat_peer, lon_peer):
            @pl.when((lat_peer > 1) | (lon_peer > 0))
            def _():
                to(lat_peer, lon_peer)

        visit = unless_corner if corner_first else to
        each_peer(lat, lon, visit, first=False)
        each_peer(lat, lon, visit, rest=False)
        return pltpu.make_async_copy(
            source.at[lon, :, lat], landing.at[pl.ds(mine, OWN)], load.at[k]
        )

    others = gate.at[pl.ds(0, CHANNELS - OWN)]

    def wait_for(semaphore):
        pltpu.make_async_copy(others, others, semaphore).wait()

    zonal_rows[...] = zonal[...].astype(F32)
    for j in range(OWN):
        row = jnp.concatenate(
            [zonal_rows[pl.ds(lon * OWN + j, 1), :], jnp.zeros((1, 256), F32)], axis=1
        )
        skew = pltpu.roll(
            jnp.broadcast_to(row, (COLS, 512)), 0, 1, stride=1, stride_axis=0
        )
        for d in range(3):
            block = skew[:, 256 - 128 * d : 384 - 128 * d]
            ahead[j, d * COLS : (d + 1) * COLS, :] = block.astype(BF16)
            back[j, (2 - d) * COLS : (3 - d) * COLS, :] = block.T.astype(BF16)
        line = meridional[pl.ds(lon * OWN + j, 1), :]
        turned = pltpu.roll(
            jnp.broadcast_to(line, (ROWS, COLS)), 0, 1, stride=1, stride_axis=0
        )
        lat_weights[j] = turned.astype(BF16)
    flip_cols, flip_rows = reversal(COLS), reversal(ROWS)

    spread(grad_src, grad_in, 1, first=False)

    signal_view = signal_in.reshape(LONS, OWN, ROWS, COLS)
    grad_view = grad_in.reshape(LONS, OWN, ROWS, COLS)
    conv_view = conv_src.reshape(LONS, OWN, ROWS, COLS)
    result_view = result_src.reshape(LONS, OWN, ROWS, COLS)

    wait_for(recv.at[0])
    backwards, flipped = [], []
    for j in range(OWN):
        blocks = [signal_view[b, j] for b in range(LONS)]
        filtered = dot(around_circle(blocks), ahead[j]).astype(BF16)
        wide = jnp.concatenate(
            [filtered[b * ROWS : (b + 1) * ROWS] for b in range(LONS)], axis=1
        )
        convolved = dot(lat_weights[j][:, :ROWS], wide, 0, 0).astype(BF16)
        for b in range(LONS):
            conv_view[b, j] = convolved[:, b * COLS : (b + 1) * COLS]
        flipped.append(dot(flip_rows, wide).astype(BF16))
    own_conv = give_back(conv_src, conv_in, 2)
    own_conv.start()
    for j in range(OWN):
        stack = jnp.concatenate([signal_view[b, j] for b in range(LONS)], axis=0)
        turned = dot(stack, flip_cols).astype(BF16)
        backwards.append([turned[b * ROWS : (b + 1) * ROWS] for b in range(LONS)])

    wait_for(recv.at[1])
    rounded = []
    for j in range(OWN):
        wide = jnp.concatenate([grad_view[b, j] for b in range(LONS)], axis=1)
        gradient = dot(lat_weights[j][:, :ROWS], wide).astype(BF16)
        blocks = [gradient[:, b * COLS : (b + 1) * COLS] for b in range(LONS)]
        rounded.append(jnp.concatenate(blocks, axis=0))
        result = dot(around_circle(blocks), back[j]).astype(BF16)
        for b in range(LONS):
            result_view[b, j] = result[b * ROWS : (b + 1) * ROWS]
    own_grad = give_back(result_src, grad_out, 3, corner_first=True)
    own_grad.start()

    scale = 1.0 / 256.0
    for j in range(OWN):
        products = dot(around_circle(backwards[j]), rounded[j], 0, 0)
        side = jnp.concatenate(
            [products[2 * COLS :], products[COLS : 2 * COLS], products[:COLS], jnp.zeros((COLS, COLS), F32)],
            axis=1,
        )
        diagonals = pltpu.roll(side, 385, 1, stride=1, stride_axis=0)
        taps_src[pl.ds(j, 1), :256] = (
            jnp.sum(diagonals[:, :256], axis=0, keepdims=True) * scale
        )
        wide = jnp.concatenate([grad_view[b, j] for b in range(LONS)], axis=1)
        crossed = dot(flipped[j], wide, 1, 1)
        crossed = jnp.concatenate([crossed, jnp.zeros((ROWS, ROWS), F32)], axis=1)
        diagonals = pltpu.roll(crossed, 65, 1, stride=1, stride_axis=0)
        taps_src[pl.ds(j, 1), 256:] = jnp.sum(diagonals, axis=0, keepdims=True) * scale
    for step in range(1, LONS):
        pltpu.make_async_remote_copy(
            taps_src,
            taps_in.at[lon],
            send.at[4],
            recv.at[4],
            device_id=(lat, (lon + step) % LONS),
            device_id_type=MESH,
        ).start()
    taps_in[lon] = taps_src[...]

    seven = taps_in.at[pl.ds(0, LONS - 1)]
    pltpu.make_async_copy(seven, seven, recv.at[4]).wait()
    for b in range(LONS):
        for j in range(OWN):
            zonal_out[b * OWN + j : b * OWN + j + 1, :] = taps_in[b, j : j + 1, :256]
            meridional_out[b * OWN + j : b * OWN + j + 1, :] = taps_in[b, j : j + 1, 256:]

    own_conv.wait()
    wait_for(recv.at[2])
    convolved = conv_in.reshape(*flat)[...].astype(F32)
    mixed_out.reshape(*flat)[...] = (gate_flat[...].astype(F32) * convolved).astype(BF16)
    gate_out.reshape(*flat)[...] = (cotangent_flat[...].astype(F32) * convolved).astype(BF16)
    own_grad.wait()
    wait_for(recv.at[3])
    for k in range(4):
        wait_for(send.at[k])
    pltpu.make_async_copy(seven, seven, send.at[4]).wait()


def place_results(*refs):
    count = len(refs) // 2
    copies = [
        pltpu.make_async_copy(refs[k], refs[count + k], refs[-1].at[k])
        for k in range(count)
    ]
    for copy in copies:
        copy.start()
    for copy in copies:
        copy.wait()


def on_device(signal, gate, cotangent, zonal, meridional):
    field = (CHANNELS, 2, COLS)
    pencil = (LONS, OWN, LATS, 2, COLS)
    in_vmem = pl.BlockSpec(memory_space=pltpu.VMEM)
    in_hbm = pl.BlockSpec(memory_space=pltpu.HBM)
    results = [
        (field, BF16),
        (field, BF16),
        (field, BF16),
        ((GROUP, 256), F32),
        ((GROUP, 128), F32),
    ]
    inputs = [
        pltpu.with_memory_space_constraint(array, pltpu.HBM)
        for array in (signal, gate, cotangent, zonal, meridional)
    ]
    made = pl.pallas_call(
        mixer,
        out_shape=[pltpu.VMEM(*result) for result in results],
        in_specs=[in_hbm] * 5,
        out_specs=[in_vmem] * 5,
        scratch_shapes=[
            pltpu.VMEM(field, BF16),
            pltpu.VMEM(field, BF16),
            pltpu.VMEM((GROUP, 256), BF16),
            pltpu.VMEM((GROUP, 128), F32),
            pltpu.VMEM(field, BF16),
            pltpu.VMEM((GROUP, 256), F32),
            pltpu.VMEM(field, BF16),
            pltpu.VMEM(pencil, BF16),
            pltpu.VMEM(pencil, BF16),
            pltpu.VMEM(pencil, BF16),
            pltpu.VMEM(pencil, BF16),
            pltpu.VMEM((OWN, 3 * COLS, COLS), BF16),
            pltpu.VMEM((OWN, 3 * COLS, COLS), BF16),
            pltpu.VMEM((OWN, ROWS, COLS), BF16),
            pltpu.VMEM((8, 384), F32),
            pltpu.VMEM((LONS, 8, 384), F32),
            pltpu.SemaphoreType.DMA((5,)),
            pltpu.SemaphoreType.DMA((5,)),
            pltpu.SemaphoreType.DMA((5,)),
            pltpu.SemaphoreType.REGULAR,
        ],
        compiler_params=pltpu.CompilerParams(
            collective_id=0, has_side_effects=True, vmem_limit_bytes=VMEM_BYTES
        ),
        name="mixer",
    )(*inputs)
    return pl.pallas_call(
        place_results,
        out_shape=[pltpu.HBM(*result) for result in results],
        in_specs=[in_vmem] * 5,
        out_specs=[in_hbm] * 5,
        scratch_shapes=[pltpu.SemaphoreType.DMA((5,))],
        compiler_params=pltpu.CompilerParams(vmem_limit_bytes=VMEM_BYTES),
        name="place_results",
    )(*[pltpu.with_memory_space_constraint(array, pltpu.VMEM) for array in made])


def solution(mesh):
    fields = P(None, "lat", "lon")
    filters = P("lat", None)
    return jax.shard_map(
        on_device,
        mesh=mesh,
        in_specs=(fields, fields, fields, filters, filters),
        out_specs=(fields, fields, fields, filters, filters),
        check_vma=False,
    )
```
